256 devices in a mesh: gx: 64 (over z_lo, y, x, core), row: 4 (over z_hi).
Axes of the slice: x: 4, y: 4, z: 8 (z_hi: 4, z_lo: 2; z = z_hi * 2 + z_lo), core: 2. Of those that a mesh axis runs over, the one named last changes fastest.
Arguments:
- amplitudes: float32 [1024, 4096], P('gx', 'row'), may hold values from -6 to 6
- integrals: float32 [4096, 131072], P('row', 'gx'), may hold values from -0.1875 to 0.1875
- cd_irrep: int32 [32], P('row'), may hold values from 0 to 7
- ab_irrep: int32 [1024], P('gx'), may hold values from 0 to 7
- allowed: int32 [8, 8], replicated, may hold values 0 or 1
- pair_occ: int32 [1024, 2], P(('gx', 'row')), may hold values from 0 to 99
- occ_energy: float32 [100], replicated, may hold values from -1 to -0.25
- ab_energy: float32 [131072], replicated, may hold values from 1 to 4
Outputs:
- residual: float32 [1024, 131072], P(('gx', 'row'))
- update: float32 [1024, 131072], P(('gx', 'row'))
The draws below stay inside these ranges and needn't reach their ends.
All inputs are finite; a program needn't handle non-finite values.
Results may differ from the reference program's by a relative error of at most 0.000071.
Values sent between devices are 32-bit elements; how exact they have to be, the bound alone decides.
No kernel may reach another device: no remote copies, remote signals or barrier semaphores. Data moves between devices by JAX's collectives and lax.ppermute only.
A program may use at most 128 MiB of HBM per device.

```python
import jax
import jax.numpy as jnp
from jax import lax

C = 4096
BLK = 128
NIRR = 8
NOCC = 100
AB_DEV = 2048
P_SIZE = 1024
A = 131072
NCB = 32
NAB = 1024
N_GX = 64


def set_ends(entries, stream_key, least, high):
    longest = entries.shape.index(max(entries.shape))
    spots = []
    for shift in (0, 1):
        where = [jax.random.randint(jax.random.fold_in(stream_key, axis), (), 0, length) for axis, length in enumerate(entries.shape)]
        where[longest] = (where[longest] + shift) % entries.shape[longest]
        spots.append(tuple(where))
    return entries.at[spots[0]].set(least).at[spots[1]].set(high)


def block_levels(own_key, dims, shards, least, high):
    loudness = 1.0
    for axis_at, blocks in shards:
        draws = jax.random.uniform(jax.random.fold_in(jax.random.fold_in(own_key, 6), axis_at), (blocks,), jnp.float32, least / len(shards), high / len(shards))
        loudness = loudness * jnp.repeat(jnp.exp(draws), dims[axis_at] // blocks).reshape((-1,) + (1,) * (len(dims) - 1 - axis_at))
    return loudness


def centred(rng, dims, scale, limit, pieces=(), kind=jnp.bfloat16):
    entries = scale * jax.random.normal(rng, dims, jnp.float32)
    if pieces:
        entries = entries * block_levels(rng, dims, pieces, -0.22, 0.18)
    return jnp.clip(entries, -limit, limit).astype(kind)


def setup_inputs(seed: int = 0) -> dict:
    key_list = jax.random.split(jax.random.key(seed), 9)
    return {
        "amplitudes": centred(key_list[0], (P_SIZE, C), 1.0, 6.0, ((0, 64), (1, 4)), jnp.float32),
        "integrals": centred(key_list[1], (C, A), (C // 4) ** -0.5, 0.1875, ((0, 4), (1, 64)), jnp.float32),
        "cd_irrep": set_ends(jax.random.randint(key_list[2], (NCB,), 0, NIRR), jax.random.fold_in(key_list[2], 1), 0, NIRR - 1).astype(jnp.int32),
        "ab_irrep": set_ends(jax.random.randint(key_list[3], (NAB,), 0, NIRR), jax.random.fold_in(key_list[3], 1), 0, NIRR - 1).astype(jnp.int32),
        "allowed": set_ends((jax.random.randint(key_list[4], (NIRR, NIRR), 0, 4) < 1).astype(jnp.int32), jax.random.fold_in(key_list[4], 1), 0, 1),
        "pair_occ": set_ends(jax.random.randint(key_list[5], (P_SIZE, 2), 0, NOCC), jax.random.fold_in(key_list[5], 1), 0, NOCC - 1).astype(jnp.int32),
        "occ_energy": jnp.clip(jax.random.uniform(key_list[6], (NOCC,), jnp.float32, -1.0, -0.25), -1.0, -0.25),
        "ab_energy": jnp.clip(jax.random.uniform(key_list[7], (A,), jnp.float32, 1.0, 4.0), 1.0, 4.0),
    }


def reference(amplitudes, integrals, cd_irrep, ab_irrep, allowed, pair_occ, occ_energy, ab_energy):
    block_mask = allowed[cd_irrep[:, None], ab_irrep[None, :]].astype(jnp.float32)
    ab_blocks = AB_DEV // BLK

    def one_slab(index):
        columns = lax.dynamic_slice_in_dim(integrals, index * AB_DEV, AB_DEV, 1)
        mask_part = lax.dynamic_slice_in_dim(block_mask, index * ab_blocks, ab_blocks, 1)
        effective = (columns.reshape(NCB, BLK, ab_blocks, BLK) * mask_part[:, None, :, None]).reshape(C, AB_DEV)
        return jnp.dot(amplitudes, effective, precision=lax.Precision.HIGHEST, preferred_element_type=jnp.float32)

    slabs = lax.map(one_slab, jnp.arange(N_GX, dtype=jnp.int32))
    residual = slabs.transpose(1, 0, 2).reshape(P_SIZE, A)
    pair_energy = occ_energy[pair_occ[:, 0]] + occ_energy[pair_occ[:, 1]]
    update = residual / (ab_energy[None, :] - pair_energy[:, None])
    return residual, update
```

```python
import jax
import jax.numpy as jnp
from jax import lax
from jax.sharding import Mesh, PartitionSpec as P

BLK = 128
GX = ("zl", "y", "x", "c")
PLANE = ("y", "x", "c")
Z = ("zl", "row")
NCHUNK = 4


def z_shift(value, shift):
    at = [4 * (z % 2) + z // 2 for z in range(8)]
    return lax.ppermute(value, Z, [(at[z], at[(z + shift) % 8]) for z in range(8)])


def split_bf16(value):
    high = lax.reduce_precision(value, 8, 7)
    return high.astype(jnp.bfloat16), (value - high).astype(jnp.bfloat16)


def body(amplitudes, integrals, cd_irrep, ab_irrep, allowed, pair_occ, occ_energy, ab_energy):
    zl = lax.axis_index("zl")
    row = lax.axis_index("row")
    depth = amplitudes.shape[1]
    cols = integrals.shape[1]
    per = 4 // NCHUNK

    labels = jnp.arange(allowed.shape[0], dtype=jnp.int32)
    cd_hot = (cd_irrep[:, None] == labels[None, :])[:, None, :, None]
    ab_hot = (ab_irrep[:, None] == labels[None, :])[None, :, None, :]
    block_mask = jnp.sum(jnp.where(cd_hot & ab_hot, allowed[None, None], 0), axis=(2, 3)).astype(jnp.float32)
    effective = (
        integrals.reshape(depth // BLK, BLK, cols // BLK, BLK) * block_mask[:, None, :, None]
    ).reshape(depth, cols)
    int_high, int_low = split_bf16(effective)
    right_side = jnp.concatenate([int_high, int_low, int_high], axis=0)

    own = amplitudes.reshape(4, NCHUNK, per, depth)
    rel = lax.dynamic_slice_in_dim(jnp.concatenate([own, own], axis=0), row, 4, 0)
    rel = rel.transpose(1, 0, 2, 3)
    same = rel
    for_one = jnp.stack([rel[:, 2], rel[:, 3], rel[:, 1], rel[:, 0]], axis=1)
    for_zero = jnp.stack([rel[:, 1], rel[:, 2], rel[:, 0], rel[:, 3]], axis=1)
    cross = lax.ppermute(jnp.where(zl == 0, for_one, for_zero), "zl", [(0, 1), (1, 0)])
    both = jnp.concatenate([same, cross], axis=1)

    def gathered(part):
        n = part.shape[0]
        flat = part.reshape(1, n * 8 * per, depth)
        sent = jnp.broadcast_to(flat, (32, n * 8 * per, depth))
        got = lax.all_to_all(sent, PLANE, 0, 0, tiled=True)
        return got.reshape(32, n, 8, per, depth)

    first = gathered(both[:1])
    rest = gathered(both[1:])

    def left_side(got):
        t = got.transpose(1, 2, 0, 3)
        s = t[:4]
        c = t[4:].reshape(4, per * 32, depth)
        h1 = s[:, :, :16].reshape(4, per * 16, depth)
        h2 = s[:, :, 16:].reshape(4, per * 16, depth)
        rows = jnp.concatenate(
            [h2[2], c[0], h1[2], c[1], h1[1], h2[3], h2[1], c[2], h1[3], c[3], h1[0], h2[0]], axis=0
        )
        high, low = split_bf16(rows)
        return jnp.concatenate([high, high, low], axis=1)

    def summed(got):
        x = jnp.dot(left_side(got), right_side, preferred_element_type=jnp.float32)
        u = 16 * per
        right1 = z_shift(x[: 3 * u], 2)
        left1 = z_shift(x[3 * u : 6 * u], -2)
        direct_right = z_shift(x[6 * u : 7 * u], 2)
        direct_left = z_shift(x[7 * u : 8 * u], -2)
        to_right = x[8 * u : 11 * u] + right1
        to_left = x[11 * u : 14 * u] + left1
        relay_right = z_shift(to_right[:u], 2)
        relay_left = z_shift(to_left[:u], -2)
        cross_right = z_shift(to_right[u:], 1)
        cross_left = z_shift(to_left[u:], -1)
        own_h1 = x[14 * u : 15 * u] + direct_right + relay_left
        own_h2 = x[15 * u :] + direct_left + relay_right
        own_sum = jnp.concatenate(
            [own_h1.reshape(per, 16, cols), own_h2.reshape(per, 16, cols)], axis=1
        )
        cross_sum = (cross_right + cross_left).reshape(per, 32, cols)
        pair = jnp.stack(
            [jnp.where(zl == 0, own_sum, cross_sum), jnp.where(zl == 0, cross_sum, own_sum)], axis=0
        )
        sent = pair.transpose(2, 1, 0, 3).reshape(32, per * 2 * cols // BLK, BLK)
        got = lax.all_to_all(sent, PLANE, 0, 0, tiled=True)
        return got.reshape(32, per, 2, cols).transpose(1, 2, 0, 3).reshape(per, 64 * cols)

    parts = [summed(first[:, 0])] + [summed(rest[:, k]) for k in range(NCHUNK - 1)]
    residual = jnp.concatenate(parts, axis=0)

    occ_labels = jnp.arange(occ_energy.shape[0], dtype=jnp.int32)
    pair_hot = (pair_occ[:, :, None] == occ_labels[None, None, :]).astype(jnp.float32)
    pair_energy = jnp.sum(pair_hot * occ_energy[None, None, :], axis=(1, 2))
    update = residual / (ab_energy[None, :] - pair_energy[:, None])
    return (residual, update)


def solution(mesh):
    fine = Mesh(mesh.devices.reshape(2, 4, 4, 2, 4), GX + ("row",))
    return jax.shard_map(
        body,
        mesh=fine,
        in_specs=(
            P(GX, "row"),
            P("row", GX),
            P("row"),
            P(GX),
            P(),
            P(GX + ("row",), None),
            P(),
            P(),
        ),
        out_specs=(P(GX + ("row",), None), P(GX + ("row",), None)),
        check_vma=False,
    )
```

```python
import jax
import jax.numpy as jnp
from jax import lax
from jax.experimental import pallas as pl
from jax.experimental.pallas import tpu as pltpu
from jax.sharding import Mesh, PartitionSpec as P

BLK = 128
TILE = 512
STEP = 256
GX = ("zl", "y", "x", "c")
PLANE = ("y", "x", "c")
Z = ("zl", "row")


def z_shift(value, shift):
    at = [4 * (z % 2) + z // 2 for z in range(8)]
    return lax.ppermute(value, Z, [(at[z], at[(z + shift) % 8]) for z in range(8)])


def ring(axis, value, shift):
    return lax.ppermute(value, axis, [((i + shift) % 4, i) for i in range(4)])


def gate(values, earlier):
    anywhere = pl.BlockSpec(memory_space=pl.ANY)
    return pl.pallas_call(
        lambda *refs: None,
        in_specs=[anywhere] * (len(values) + len(earlier)),
        out_specs=[anywhere] * len(values),
        out_shape=[jax.ShapeDtypeStruct(value.shape, value.dtype) for value in values],
        input_output_aliases={k: k for k in range(len(values))},
        cost_estimate=pl.CostEstimate(flops=0, bytes_accessed=0, transcendentals=0),
    )(*values, *earlier)


def pack(half, place, near, far, earlier):
    cols = near[0].shape[-1]
    chunks = cols // BLK

    def kernel(place_ref, own_n, other_n, own_f, right_f, left_f, *refs):
        out_ref = refs[-1]
        here = lax.rem(pl.program_id(0) - place_ref[0] + 4, 4) == 0
        for i in range(2):
            own = jnp.where(here, own_n[i], own_f[i, 0])
            other = jnp.where(here, other_n[i], right_f[i, 0] + left_f[i, 0])
            for z in range(2):
                value = jnp.where(place_ref[1] == z, own, other)
                for k in range(chunks):
                    out_ref[:, (2 * i + z) * chunks + k, :] = value[:, k * BLK : (k + 1) * BLK]

    near_spec = pl.BlockSpec((2, 8, cols), lambda j, place: (half, 0, 0))
    far_spec = pl.BlockSpec(
        (2, 1, 8, cols), lambda j, place: (0, jnp.maximum(lax.rem(j - place[0] + 4, 4) - 1, 0), 0, 0)
    )
    return pl.pallas_call(
        kernel,
        grid_spec=pltpu.PrefetchScalarGridSpec(
            num_scalar_prefetch=1,
            grid=(4,),
            in_specs=[near_spec] * 2 + [far_spec] * 3 + [pl.BlockSpec(memory_space=pl.ANY)] * len(earlier),
            out_specs=pl.BlockSpec((8, 4 * chunks, BLK), lambda j, place: (j, 0, 0)),
        ),
        out_shape=jax.ShapeDtypeStruct((32, 4 * chunks, BLK), jnp.float32),
        cost_estimate=pl.CostEstimate(flops=0, bytes_accessed=2**20, transcendentals=0),
    )(place, *near, *far, *earlier)


def multiply(pieces, order, integrals, mask_rows, sizes, earlier=()):
    rows = order.shape[0]
    depth, cols = integrals.shape
    tile = min(TILE, cols)
    step = min(STEP, tile)

    def kernel(*refs):
        piece_refs, refs = refs[: len(pieces)], refs[len(pieces) :]
        order_ref, int_ref, mask_ref = refs[:3]
        out_refs, (high_ref, low_ref) = refs[3 + len(earlier) : -2], refs[-2:]

        @pl.when(pl.program_id(0) == 0)
        def _():
            value = jnp.concatenate([ref[...] for ref in piece_refs], axis=0)
            high = value.astype(jnp.bfloat16)
            low = (value - high.astype(jnp.float32)).astype(jnp.bfloat16)
            for part, part_ref in ((high, high_ref), (low, low_ref)):
                moved = jnp.dot(order_ref[...], part, preferred_element_type=jnp.float32)
                part_ref[...] = moved.astype(jnp.bfloat16)

        for start in range(0, tile, step):
            here = slice(start, start + step)
            effective = jnp.concatenate(
                [
                    int_ref[b * BLK : (b + 1) * BLK, here] * mask_ref[b : b + 1, here]
                    for b in range(depth // BLK)
                ],
                axis=0,
            )
            high = effective.astype(jnp.bfloat16)
            low = (effective - high.astype(jnp.float32)).astype(jnp.bfloat16)
            total = jnp.dot(high_ref[...], low, preferred_element_type=jnp.float32)
            total += jnp.dot(low_ref[...], high, preferred_element_type=jnp.float32)
            total += jnp.dot(high_ref[...], high, preferred_element_type=jnp.float32)
            at = 0
            for size, out_ref in zip(sizes, out_refs):
                out_ref[:, here] = total[at : at + size]
                at += size

    return pl.pallas_call(
        kernel,
        grid=(cols // tile,),
        in_specs=[pl.BlockSpec(piece.shape, lambda j: (0, 0)) for piece in pieces]
        + [
            pl.BlockSpec(order.shape, lambda j: (0, 0)),
            pl.BlockSpec((depth, tile), lambda j: (0, j)),
            pl.BlockSpec((mask_rows.shape[0], tile), lambda j: (0, j)),
        ]
        + [pl.BlockSpec(memory_space=pl.ANY)] * len(earlier),
        out_specs=[pl.BlockSpec((size, tile), lambda j: (0, j)) for size in sizes],
        out_shape=[jax.ShapeDtypeStruct((size, cols), jnp.float32) for size in sizes],
        scratch_shapes=[pltpu.VMEM((rows, depth), jnp.bfloat16)] * 2,
        compiler_params=pltpu.CompilerParams(vmem_limit_bytes=56 * 2**20),
        cost_estimate=pl.CostEstimate(
            flops=6 * rows * depth * cols,
            bytes_accessed=4 * (rows * depth + depth * cols + rows * cols),
            transcendentals=0,
        ),
    )(*pieces, order, integrals, mask_rows, *earlier)


def body(amplitudes, integrals, cd_irrep, ab_irrep, allowed, pair_occ, occ_energy, ab_energy):
    zl = lax.axis_index("zl")
    row = lax.axis_index("row")
    y, x, c = lax.axis_index("y"), lax.axis_index("x"), lax.axis_index("c")
    depth = amplitudes.shape[1]
    cols = integrals.shape[1]

    labels = jnp.arange(allowed.shape[0], dtype=jnp.int32)
    cd_hot = (cd_irrep[:, None] == labels[None, :])[:, None, :, None]
    ab_hot = (ab_irrep[:, None] == labels[None, :])[None, :, None, :]
    block_mask = jnp.sum(jnp.where(cd_hot & ab_hot, allowed[None, None], 0), axis=(2, 3)).astype(jnp.float32)
    mask_rows = jnp.repeat(block_mask, BLK, axis=1)

    mine = amplitudes.reshape(4, 2, 2, depth).transpose(1, 0, 2, 3).reshape(2, 8, depth)
    theirs = lax.ppermute(mine, "zl", [(0, 1), (1, 0)])
    flat = jnp.concatenate([mine, theirs], axis=1)
    in_x = jnp.stack([flat] + [ring("x", flat, shift) for shift in (1, 2, 3)], axis=0)

    def other_core(value):
        return lax.ppermute(value, "c", [(0, 1), (1, 0)])

    def order_of(source, total):
        found = source.reshape(-1, 1) == jnp.arange(total, dtype=jnp.int32)[None, :]
        return found.astype(jnp.bfloat16)

    def iotas(*grid):
        return [lax.broadcasted_iota(jnp.int32, grid, k) for k in range(len(grid))]

    def near_order():
        r, s, h, i, _, at_x, at_c = iotas(4, 2, 2, 2, 1, 4, 2)
        piece = jnp.where(at_c == c, 0, 1)
        dx = lax.rem(at_x - x + 4, 4)
        return order_of(((((piece * 4 + dx) * 2 + h) * 2 + s) * 4 + r) * 2 + i, 256)

    def far_order():
        o, i, dy, at_x, at_c = iotas(8, 2, 3, 4, 2)
        steps = [jnp.where(zl == 0, zero, one) for zero, one in ((1, 2), (2, 3), (0, 1), (3, 0))]
        r = o
        for k in range(4):
            r = jnp.where(o == 4 + k, lax.rem(row + steps[k], 4), r)
        s = jnp.where(o < 4, 0, 1)
        piece = jnp.where(at_c == c, 0, 3) + dy
        dx = lax.rem(at_x - x + 4, 4)
        return order_of((((piece * 4 + dx) * 2 + s) * 4 + r) * 2 + i, 384)

    def last_order():
        steps = [jnp.where(zl == 0, zero, one) for zero, one in ((1, 2), (2, 3), (0, 1), (3, 0))]
        groups = (
            [(0, 2, 1), (1, 0, 0), (1, 0, 1), (0, 1, 0)]
            + [(0, 2, 0), (1, 1, 0), (1, 1, 1), (0, 3, 1)]
            + [(0, 1, 1), (1, 2, 0), (1, 2, 1)]
            + [(0, 3, 0), (1, 3, 0), (1, 3, 1)]
            + [(0, 0, 0), (0, 0, 1)]
        )
        starts = [
            (s * 4 + lax.rem(row + (steps[k] if s else k), 4)) * 2 + i for s, k, i in groups
        ]
        start = jnp.stack(starts).astype(jnp.int32).reshape(16, 1, 1, 1)
        _, dy, at_x, at_c = iotas(16, 3, 4, 2)
        piece = jnp.where(at_c == c, 0, 3) + dy
        return order_of((piece * 4 + lax.rem(at_x - x + 4, 4)) * 16 + start, 384)

    def product(pieces, order, sizes, *earlier):
        return multiply(pieces, order, integrals, mask_rows, sizes, earlier)

    def own_sum(part):
        return lax.psum_scatter(part[0], "row", scatter_dimension=0, tiled=True)

    def first_stage(part):
        return z_shift(part[1], 2), z_shift(part[2], -2)

    def second_stage(part, got):
        return z_shift(part[3] + got[0], 1), z_shift(part[4] + got[1], -1)

    def packed(half, near_sums, far_sums, earlier=()):
        near_sums = [value.reshape(4, 8, cols) for value in near_sums]
        far_sums = [value.reshape(2, 3, 8, cols) for value in far_sums]
        return pack(half, jnp.stack([y, zl]).astype(jnp.int32), near_sums, far_sums, earlier)

    def to_owners(sent):
        return lax.all_to_all(sent, PLANE, 0, 0, tiled=True)

    pieces = in_x.reshape(128, depth)
    part_near = product([pieces, other_core(pieces)], near_order(), (256,))
    sum_near = own_sum(part_near)
    sums_near = (sum_near[:32], lax.ppermute(sum_near[32:], "zl", [(0, 1), (1, 0)]))

    order = far_order()
    sizes = (192, 48, 48, 48, 48)

    def gathered(half, before, after):
        pieces = in_x[:, half].reshape(64, depth)
        if before:
            (pieces,) = gate([pieces], before)
        pieces = list(gate([ring("y", pieces, shift) for shift in (1, 2, 3)], after))
        return pieces + [other_core(value) for value in pieces]

    far_a = gathered(0, (), part_near)
    part_a = product(far_a, order, sizes)
    own_a = own_sum(part_a)
    first_a = first_stage(part_a)

    far_b = gathered(1, far_a[:3], part_a[1:2])
    part_b = product(far_b, last_order(), (96, 96, 72, 72, 48), *first_a)
    first_b = first_stage((None, *part_b[:2]))
    out_a = to_owners(packed(0, sums_near, (own_a,) + second_stage(part_a, first_a), first_b))

    right, left = first_b
    to_right = part_b[2] + right[:72]
    to_left = part_b[3] + left[:72]
    relay_right, cross_right = z_shift(to_right[:24], 2), z_shift(to_right[24:], 1)
    relay_left, cross_left = z_shift(to_left[:24], -2), z_shift(to_left[24:], -1)
    own_b = jnp.concatenate(
        [part_b[4][:24] + right[72:] + relay_left, part_b[4][24:] + left[72:] + relay_right], axis=0
    )
    out_b = to_owners(packed(1, sums_near, (own_b, cross_right, cross_left)))
    out = [
        got.reshape(32, 2, 2, cols).transpose(1, 2, 0, 3).reshape(2, 64 * cols) for got in (out_a, out_b)
    ]

    residual = jnp.concatenate(out, axis=0)
    occ_labels = jnp.arange(occ_energy.shape[0], dtype=jnp.int32)
    pair_hot = (pair_occ[:, :, None] == occ_labels[None, None, :]).astype(jnp.float32)
    pair_energy = jnp.sum(pair_hot * occ_energy[None, None, :], axis=(1, 2))
    update = residual / (ab_energy[None, :] - pair_energy[:, None])
    return (residual, update)


def solution(mesh):
    fine = Mesh(mesh.devices.reshape(2, 4, 4, 2, 4), GX + ("row",))
    return jax.shard_map(
        body,
        mesh=fine,
        in_specs=(
            P(GX, "row"),
            P("row", GX),
            P("row"),
            P(GX),
            P(),
            P(GX + ("row",), None),
            P(),
            P(),
        ),
        out_specs=(P(GX + ("row",), None), P(GX + ("row",), None)),
        check_vma=False,
    )
```

```python
import jax
import jax.numpy as jnp
from jax import lax
from jax.experimental import pallas as pl
from jax.experimental.pallas import tpu as pltpu
from jax.sharding import Mesh, PartitionSpec as P

BLK = 128
TILE = 512
STEP = 256
GX = ("zl", "y", "x", "c")
PLANE = ("y", "x", "c")
Z = ("zl", "row")


def z_shift(value, shift):
    at = [4 * (z % 2) + z // 2 for z in range(8)]
    return lax.ppermute(value, Z, [(at[z], at[(z + shift) % 8]) for z in range(8)])


def ring(axis, value, shift):
    return lax.ppermute(value, axis, [((i + shift) % 4, i) for i in range(4)])


def gate(values, earlier):
    anywhere = pl.BlockSpec(memory_space=pl.ANY)
    return pl.pallas_call(
        lambda *refs: None,
        in_specs=[anywhere] * (len(values) + len(earlier)),
        out_specs=[anywhere] * len(values),
        out_shape=[jax.ShapeDtypeStruct(value.shape, value.dtype) for value in values],
        input_output_aliases={k: k for k in range(len(values))},
        cost_estimate=pl.CostEstimate(flops=0, bytes_accessed=0, transcendentals=0),
    )(*values, *earlier)


def pack(half, place, near, far, earlier):
    cols = near[0].shape[-1]
    chunks = cols // BLK

    def kernel(place_ref, own_n, other_n, own_f, right_f, left_f, *refs):
        out_ref = refs[-1]
        here = lax.rem(pl.program_id(0) - place_ref[0] + 4, 4) == 0
        for i in range(2):
            own = jnp.where(here, own_n[i], own_f[i, 0])
            other = jnp.where(here, other_n[i], right_f[i, 0] + left_f[i, 0])
            for z in range(2):
                value = jnp.where(place_ref[1] == z, own, other)
                for k in range(chunks):
                    out_ref[:, (2 * i + z) * chunks + k, :] = value[:, k * BLK : (k + 1) * BLK]

    near_spec = pl.BlockSpec((2, 8, cols), lambda j, place: (half, 0, 0))
    far_spec = pl.BlockSpec(
        (2, 1, 8, cols), lambda j, place: (0, jnp.maximum(lax.rem(j - place[0] + 4, 4) - 1, 0), 0, 0)
    )
    return pl.pallas_call(
        kernel,
        grid_spec=pltpu.PrefetchScalarGridSpec(
            num_scalar_prefetch=1,
            grid=(4,),
            in_specs=[near_spec] * 2 + [far_spec] * 3 + [pl.BlockSpec(memory_space=pl.ANY)] * len(earlier),
            out_specs=pl.BlockSpec((8, 4 * chunks, BLK), lambda j, place: (j, 0, 0)),
        ),
        out_shape=jax.ShapeDtypeStruct((32, 4 * chunks, BLK), jnp.float32),
        cost_estimate=pl.CostEstimate(flops=0, bytes_accessed=2**20, transcendentals=0),
    )(place, *near, *far, *earlier)


def multiply(pieces, order, integrals, mask_rows, sizes, earlier=()):
    rows = order.shape[0]
    depth, cols = integrals.shape
    tile = min(TILE, cols)
    step = min(STEP, tile)

    def kernel(*refs):
        piece_refs, refs = refs[: len(pieces)], refs[len(pieces) :]
        order_ref, int_ref, mask_ref = refs[:3]
        out_refs, (high_ref, low_ref) = refs[3 + len(earlier) : -2], refs[-2:]

        @pl.when(pl.program_id(0) == 0)
        def _():
            value = jnp.concatenate([ref[...] for ref in piece_refs], axis=0)
            high = value.astype(jnp.bfloat16)
            low = (value - high.astype(jnp.float32)).astype(jnp.bfloat16)
            for part, part_ref in ((high, high_ref), (low, low_ref)):
                moved = jnp.dot(order_ref[...], part, preferred_element_type=jnp.float32)
                part_ref[...] = moved.astype(jnp.bfloat16)

        for start in range(0, tile, step):
            here = slice(start, start + step)
            effective = jnp.concatenate(
                [
                    int_ref[b * BLK : (b + 1) * BLK, here] * mask_ref[b : b + 1, here]
                    for b in range(depth // BLK)
                ],
                axis=0,
            )
            high = effective.astype(jnp.bfloat16)
            low = (effective - high.astype(jnp.float32)).astype(jnp.bfloat16)
            total = jnp.dot(high_ref[...], low, preferred_element_type=jnp.float32)
            total += jnp.dot(low_ref[...], high, preferred_element_type=jnp.float32)
            total += jnp.dot(high_ref[...], high, preferred_element_type=jnp.float32)
            at = 0
            for size, out_ref in zip(sizes, out_refs):
                out_ref[:, here] = total[at : at + size]
                at += size

    return pl.pallas_call(
        kernel,
        grid=(cols // tile,),
        in_specs=[pl.BlockSpec(piece.shape, lambda j: (0, 0)) for piece in pieces]
        + [
            pl.BlockSpec(order.shape, lambda j: (0, 0)),
            pl.BlockSpec((depth, tile), lambda j: (0, j)),
            pl.BlockSpec((mask_rows.shape[0], tile), lambda j: (0, j)),
        ]
        + [pl.BlockSpec(memory_space=pl.ANY)] * len(earlier),
        out_specs=[pl.BlockSpec((size, tile), lambda j: (0, j)) for size in sizes],
        out_shape=[jax.ShapeDtypeStruct((size, cols), jnp.float32) for size in sizes],
        scratch_shapes=[pltpu.VMEM((rows, depth), jnp.bfloat16)] * 2,
        compiler_params=pltpu.CompilerParams(vmem_limit_bytes=56 * 2**20),
        cost_estimate=pl.CostEstimate(
            flops=6 * rows * depth * cols,
            bytes_accessed=4 * (rows * depth + depth * cols + rows * cols),
            transcendentals=0,
        ),
    )(*pieces, order, integrals, mask_rows, *earlier)


def body(amplitudes, integrals, cd_irrep, ab_irrep, allowed, pair_occ, occ_energy, ab_energy):
    zl = lax.axis_index("zl")
    row = lax.axis_index("row")
    y, x, c = lax.axis_index("y"), lax.axis_index("x"), lax.axis_index("c")
    depth = amplitudes.shape[1]
    cols = integrals.shape[1]

    labels = jnp.arange(allowed.shape[0], dtype=jnp.int32)
    cd_hot = (cd_irrep[:, None] == labels[None, :])[:, None, :, None]
    ab_hot = (ab_irrep[:, None] == labels[None, :])[None, :, None, :]
    block_mask = jnp.sum(jnp.where(cd_hot & ab_hot, allowed[None, None], 0), axis=(2, 3)).astype(jnp.float32)
    mask_rows = jnp.repeat(block_mask, BLK, axis=1)

    mine = amplitudes.reshape(4, 2, 2, depth).transpose(1, 0, 2, 3).reshape(2, 8, depth)
    theirs = lax.ppermute(mine, "zl", [(0, 1), (1, 0)])
    flat = jnp.concatenate([mine, theirs], axis=1)
    in_x = jnp.stack([flat] + [ring("x", flat, shift) for shift in (1, 2, 3)], axis=0)

    def other_core(value):
        return lax.ppermute(value, "c", [(0, 1), (1, 0)])

    def order_of(source, total):
        found = source.reshape(-1, 1) == jnp.arange(total, dtype=jnp.int32)[None, :]
        return found.astype(jnp.bfloat16)

    def iotas(*grid):
        return [lax.broadcasted_iota(jnp.int32, grid, k) for k in range(len(grid))]

    def near_order():
        r, s, h, i, _, at_x, at_c = iotas(4, 2, 2, 2, 1, 4, 2)
        piece = jnp.where(at_c == c, 0, 1)
        dx = lax.rem(at_x - x + 4, 4)
        return order_of(((((piece * 4 + dx) * 2 + h) * 2 + s) * 4 + r) * 2 + i, 256)

    def far_order():
        o, i, dy, at_x, at_c = iotas(8, 2, 3, 4, 2)
        steps = [jnp.where(zl == 0, zero, one) for zero, one in ((1, 2), (2, 3), (0, 1), (3, 0))]
        r = o
        for k in range(4):
            r = jnp.where(o == 4 + k, lax.rem(row + steps[k], 4), r)
        s = jnp.where(o < 4, 0, 1)
        piece = jnp.where(at_c == c, 0, 3) + dy
        dx = lax.rem(at_x - x + 4, 4)
        return order_of((((piece * 4 + dx) * 2 + s) * 4 + r) * 2 + i, 384)

    def last_order():
        steps = [jnp.where(zl == 0, zero, one) for zero, one in ((1, 2), (2, 3), (0, 1), (3, 0))]
        groups = (
            [(0, 2, 1), (1, 0, 0), (1, 0, 1), (0, 1, 0)]
            + [(0, 2, 0), (1, 1, 0), (1, 1, 1), (0, 3, 1)]
            + [(0, 1, 1), (1, 2, 0), (1, 2, 1)]
            + [(0, 3, 0), (1, 3, 0), (1, 3, 1)]
            + [(0, 0, 0), (0, 0, 1)]
        )
        starts = [
            (s * 4 + lax.rem(row + (steps[k] if s else k), 4)) * 2 + i for s, k, i in groups
        ]
        start = jnp.stack(starts).astype(jnp.int32).reshape(16, 1, 1, 1)
        _, dy, at_x, at_c = iotas(16, 3, 4, 2)
        piece = jnp.where(at_c == c, 0, 3) + dy
        return order_of((piece * 4 + lax.rem(at_x - x + 4, 4)) * 16 + start, 384)

    def product(pieces, order, sizes, *earlier):
        return multiply(pieces, order, integrals, mask_rows, sizes, earlier)

    def own_sum(part):
        return lax.psum_scatter(part[0], "row", scatter_dimension=0, tiled=True)

    def first_stage(part):
        return z_shift(part[1], 2), z_shift(part[2], -2)

    def second_stage(part, got):
        return z_shift(part[3] + got[0], 1), z_shift(part[4] + got[1], -1)

    def packed(half, near_sums, far_sums, earlier=()):
        near_sums = [value.reshape(4, 8, cols) for value in near_sums]
        far_sums = [value.reshape(2, 3, 8, cols) for value in far_sums]
        return pack(half, jnp.stack([y, zl]).astype(jnp.int32), near_sums, far_sums, earlier)

    def to_owners(sent):
        return lax.all_to_all(sent, PLANE, 0, 0, tiled=True)

    pieces = in_x.reshape(128, depth)
    part_near = product([pieces, other_core(pieces)], near_order(), (256,))
    sum_near = own_sum(part_near)
    sums_near = (sum_near[:32], lax.ppermute(sum_near[32:], "zl", [(0, 1), (1, 0)]))

    order = far_order()
    sizes = (192, 48, 48, 48, 48)

    def gathered(half, before, after):
        pieces = in_x[:, half].reshape(64, depth)
        if before:
            (pieces,) = gate([pieces], before)
        pieces = list(gate([ring("y", pieces, shift) for shift in (1, 2, 3)], after))
        return pieces + [other_core(value) for value in pieces]

    far_a = gathered(0, (), part_near)
    part_a = product(far_a, order, sizes)
    own_a = own_sum(part_a)
    first_a = first_stage(part_a)

    far_b = gathered(1, far_a[:3], part_a[1:2])
    second_a = second_stage(part_a, first_a)
    part_b = product(far_b, last_order(), (96, 96, 72, 72, 48), *second_a, sums_near[1])
    first_b = first_stage((None, *part_b[:2]))
    sent_a = packed(0, sums_near, (own_a,) + second_a)
    out_a = to_owners(sent_a)

    right, left = first_b
    to_right = part_b[2] + right[:72]
    to_left = part_b[3] + left[:72]
    relay_right, cross_right = z_shift(to_right[:24], 2), z_shift(to_right[24:], 1)
    relay_left, cross_left = z_shift(to_left[:24], -2), z_shift(to_left[24:], -1)
    own_b = jnp.concatenate(
        [part_b[4][:24] + right[72:] + relay_left, part_b[4][24:] + left[72:] + relay_right], axis=0
    )
    out_b = to_owners(packed(1, sums_near, (own_b, cross_right, cross_left)))
    out = [
        got.reshape(32, 2, 2, cols).transpose(1, 2, 0, 3).reshape(2, 64 * cols) for got in (out_a, out_b)
    ]

    residual = jnp.concatenate(out, axis=0)
    occ_labels = jnp.arange(occ_energy.shape[0], dtype=jnp.int32)
    pair_hot = (pair_occ[:, :, None] == occ_labels[None, None, :]).astype(jnp.float32)
    pair_energy = jnp.sum(pair_hot * occ_energy[None, None, :], axis=(1, 2))
    update = residual / (ab_energy[None, :] - pair_energy[:, None])
    return (residual, update)


def solution(mesh):
    fine = Mesh(mesh.devices.reshape(2, 4, 4, 2, 4), GX + ("row",))
    return jax.shard_map(
        body,
        mesh=fine,
        in_specs=(
            P(GX, "row"),
            P("row", GX),
            P("row"),
            P(GX),
            P(),
            P(GX + ("row",), None),
            P(),
            P(),
        ),
        out_specs=(P(GX + ("row",), None), P(GX + ("row",), None)),
        check_vma=False,
    )
```

```python
import jax
import jax.numpy as jnp
from jax import lax
from jax.experimental import pallas as pl
from jax.experimental.pallas import tpu as pltpu
from jax.sharding import Mesh, PartitionSpec as P

BLK = 128
TILE = 512
STEP = 256
GX = ("zl", "y", "x", "c")
PLANE = ("y", "x", "c")
Z = ("zl", "row")


def z_shift(value, shift):
    at = [4 * (z % 2) + z // 2 for z in range(8)]
    return lax.ppermute(value, Z, [(at[z], at[(z + shift) % 8]) for z in range(8)])


def ring(axis, value, shift):
    return lax.ppermute(value, axis, [((i + shift) % 4, i) for i in range(4)])


def gate(values, earlier):
    anywhere = pl.BlockSpec(memory_space=pl.ANY)
    return pl.pallas_call(
        lambda *refs: None,
        in_specs=[anywhere] * (len(values) + len(earlier)),
        out_specs=[anywhere] * len(values),
        out_shape=[jax.ShapeDtypeStruct(value.shape, value.dtype) for value in values],
        input_output_aliases={k: k for k in range(len(values))},
        cost_estimate=pl.CostEstimate(flops=0, bytes_accessed=0, transcendentals=0),
    )(*values, *earlier)


def pack(half, place, near, far, earlier):
    cols = near[0].shape[-1]
    chunks = cols // BLK

    def kernel(place_ref, own_n, other_n, own_f, right_f, left_f, *refs):
        out_ref = refs[-1]
        here = lax.rem(pl.program_id(0) - place_ref[0] + 4, 4) == 0
        for i in range(2):
            own = jnp.where(here, own_n[i], own_f[i, 0])
            other = jnp.where(here, other_n[i], right_f[i, 0] + left_f[i, 0])
            for z in range(2):
                value = jnp.where(place_ref[1] == z, own, other)
                for k in range(chunks):
                    out_ref[:, (2 * i + z) * chunks + k, :] = value[:, k * BLK : (k + 1) * BLK]

    near_spec = pl.BlockSpec((2, 8, cols), lambda j, place: (half, 0, 0))
    far_spec = pl.BlockSpec(
        (2, 1, 8, cols), lambda j, place: (0, jnp.maximum(lax.rem(j - place[0] + 4, 4) - 1, 0), 0, 0)
    )
    return pl.pallas_call(
        kernel,
        grid_spec=pltpu.PrefetchScalarGridSpec(
            num_scalar_prefetch=1,
            grid=(4,),
            in_specs=[near_spec] * 2 + [far_spec] * 3 + [pl.BlockSpec(memory_space=pl.ANY)] * len(earlier),
            out_specs=pl.BlockSpec((8, 4 * chunks, BLK), lambda j, place: (j, 0, 0)),
        ),
        out_shape=jax.ShapeDtypeStruct((32, 4 * chunks, BLK), jnp.float32),
        cost_estimate=pl.CostEstimate(flops=0, bytes_accessed=2**20, transcendentals=0),
    )(place, *near, *far, *earlier)


def multiply(pieces, order, integrals, mask_rows, sizes, earlier=()):
    rows = order.shape[0]
    depth, cols = integrals.shape
    tile = min(TILE, cols)
    step = min(STEP, tile)

    def kernel(*refs):
        piece_refs, refs = refs[: len(pieces)], refs[len(pieces) :]
        order_ref, int_ref, mask_ref = refs[:3]
        out_refs, (high_ref, low_ref) = refs[3 + len(earlier) : -2], refs[-2:]

        @pl.when(pl.program_id(0) == 0)
        def _():
            value = jnp.concatenate([ref[...] for ref in piece_refs], axis=0)
            high = value.astype(jnp.bfloat16)
            low = (value - high.astype(jnp.float32)).astype(jnp.bfloat16)
            for part, part_ref in ((high, high_ref), (low, low_ref)):
                moved = jnp.dot(order_ref[...], part, preferred_element_type=jnp.float32)
                part_ref[...] = moved.astype(jnp.bfloat16)

        for start in range(0, tile, step):
            here = slice(start, start + step)
            effective = jnp.concatenate(
                [
                    int_ref[b * BLK : (b + 1) * BLK, here] * mask_ref[b : b + 1, here]
                    for b in range(depth // BLK)
                ],
                axis=0,
            )
            high = effective.astype(jnp.bfloat16)
            low = (effective - high.astype(jnp.float32)).astype(jnp.bfloat16)
            total = jnp.dot(high_ref[...], low, preferred_element_type=jnp.float32)
            total += jnp.dot(low_ref[...], high, preferred_element_type=jnp.float32)
            total += jnp.dot(high_ref[...], high, preferred_element_type=jnp.float32)
            at = 0
            for size, out_ref in zip(sizes, out_refs):
                out_ref[:, here] = total[at : at + size]
                at += size

    return pl.pallas_call(
        kernel,
        grid=(cols // tile,),
        in_specs=[pl.BlockSpec(piece.shape, lambda j: (0, 0)) for piece in pieces]
        + [
            pl.BlockSpec(order.shape, lambda j: (0, 0)),
            pl.BlockSpec((depth, tile), lambda j: (0, j)),
            pl.BlockSpec((mask_rows.shape[0], tile), lambda j: (0, j)),
        ]
        + [pl.BlockSpec(memory_space=pl.ANY)] * len(earlier),
        out_specs=[pl.BlockSpec((size, tile), lambda j: (0, j)) for size in sizes],
        out_shape=[jax.ShapeDtypeStruct((size, cols), jnp.float32) for size in sizes],
        scratch_shapes=[pltpu.VMEM((rows, depth), jnp.bfloat16)] * 2,
        compiler_params=pltpu.CompilerParams(vmem_limit_bytes=56 * 2**20),
        cost_estimate=pl.CostEstimate(
            flops=6 * rows * depth * cols,
            bytes_accessed=4 * (rows * depth + depth * cols + rows * cols),
            transcendentals=0,
        ),
    )(*pieces, order, integrals, mask_rows, *earlier)


def body(amplitudes, integrals, cd_irrep, ab_irrep, allowed, pair_occ, occ_energy, ab_energy):
    zl = lax.axis_index("zl")
    row = lax.axis_index("row")
    y, x, c = lax.axis_index("y"), lax.axis_index("x"), lax.axis_index("c")
    depth = amplitudes.shape[1]
    cols = integrals.shape[1]

    labels = jnp.arange(allowed.shape[0], dtype=jnp.int32)
    cd_hot = (cd_irrep[:, None] == labels[None, :])[:, None, :, None]
    ab_hot = (ab_irrep[:, None] == labels[None, :])[None, :, None, :]
    block_mask = jnp.sum(jnp.where(cd_hot & ab_hot, allowed[None, None], 0), axis=(2, 3)).astype(jnp.float32)
    mask_rows = jnp.repeat(block_mask, BLK, axis=1)

    theirs = lax.ppermute(amplitudes, "zl", [(0, 1), (1, 0)])
    flat = jnp.concatenate([amplitudes, theirs], axis=0)
    in_x = jnp.stack([flat] + [ring("x", flat, shift) for shift in (1, 2, 3)], axis=0)

    def other_core(value):
        return lax.ppermute(value, "c", [(0, 1), (1, 0)])

    def order_of(source, total):
        found = source.reshape(-1, 1) == jnp.arange(total, dtype=jnp.int32)[None, :]
        return found.astype(jnp.bfloat16)

    def iotas(*grid):
        return [lax.broadcasted_iota(jnp.int32, grid, k) for k in range(len(grid))]

    def near_order():
        r, s, h, i, _, at_x, at_c = iotas(4, 2, 2, 2, 1, 4, 2)
        piece = jnp.where(at_c == c, 0, 1)
        dx = lax.rem(at_x - x + 4, 4)
        return order_of(((((piece * 4 + dx) * 2 + s) * 4 + r) * 2 + h) * 2 + i, 256)

    def far_order():
        o, i, dy, at_x, at_c = iotas(8, 2, 3, 4, 2)
        steps = [jnp.where(zl == 0, zero, one) for zero, one in ((1, 2), (2, 3), (0, 1), (3, 0))]
        r = o
        for k in range(4):
            r = jnp.where(o == 4 + k, lax.rem(row + steps[k], 4), r)
        s = jnp.where(o < 4, 0, 1)
        piece = jnp.where(at_c == c, 0, 3) + dy
        dx = lax.rem(at_x - x + 4, 4)
        return order_of((((piece * 4 + dx) * 2 + s) * 4 + r) * 2 + i, 384)

    def last_order():
        steps = [jnp.where(zl == 0, zero, one) for zero, one in ((1, 2), (2, 3), (0, 1), (3, 0))]
        groups = (
            [(0, 2, 1), (1, 0, 0), (1, 0, 1), (0, 1, 0)]
            + [(0, 2, 0), (1, 1, 0), (1, 1, 1), (0, 3, 1)]
            + [(0, 1, 1), (1, 2, 0), (1, 2, 1)]
            + [(0, 3, 0), (1, 3, 0), (1, 3, 1)]
            + [(0, 0, 0), (0, 0, 1)]
        )
        starts = [
            (s * 4 + lax.rem(row + (steps[k] if s else k), 4)) * 2 + i for s, k, i in groups
        ]
        start = jnp.stack(starts).astype(jnp.int32).reshape(16, 1, 1, 1)
        _, dy, at_x, at_c = iotas(16, 3, 4, 2)
        piece = jnp.where(at_c == c, 0, 3) + dy
        return order_of((piece * 4 + lax.rem(at_x - x + 4, 4)) * 16 + start, 384)

    def product(pieces, order, sizes, *earlier):
        return multiply(pieces, order, integrals, mask_rows, sizes, earlier)

    def own_sum(part):
        return lax.psum_scatter(part[0], "row", scatter_dimension=0, tiled=True)

    def first_stage(part):
        return z_shift(part[1], 2), z_shift(part[2], -2)

    def second_stage(part, got):
        return z_shift(part[3] + got[0], 1), z_shift(part[4] + got[1], -1)

    def packed(half, near_sums, far_sums, earlier=()):
        near_sums = [value.reshape(4, 8, cols) for value in near_sums]
        far_sums = [value.reshape(2, 3, 8, cols) for value in far_sums]
        return pack(half, jnp.stack([y, zl]).astype(jnp.int32), near_sums, far_sums, earlier)

    def to_owners(sent):
        return lax.all_to_all(sent, PLANE, 0, 0, tiled=True)

    pieces = in_x.reshape(128, depth)
    part_near = product([pieces, other_core(pieces)], near_order(), (256,))
    sum_near = own_sum(part_near)
    sums_near = (sum_near[:32], lax.ppermute(sum_near[32:], "zl", [(0, 1), (1, 0)]))

    order = far_order()
    sizes = (192, 48, 48, 48, 48)

    def gathered(half, before, after):
        pieces = in_x.reshape(4, 8, 2, 2, depth)[:, :, half].reshape(64, depth)
        if before:
            (pieces,) = gate([pieces], before)
        pieces = [ring("y", pieces, shift) for shift in (1, 2, 3)]
        if after:
            pieces = list(gate(pieces, after))
        return pieces + [other_core(value) for value in pieces]

    far_a = gathered(0, (), ())
    part_a = product(far_a, order, sizes, *part_near)
    own_a = own_sum(part_a)
    first_a = first_stage(part_a)

    far_b = gathered(1, far_a[:3], part_a[1:2])
    second_a = second_stage(part_a, first_a)
    part_b = product(far_b, last_order(), (96, 96, 72, 72, 48), *second_a)
    first_b = first_stage((None, *part_b[:2]))
    sent_a = packed(0, sums_near, (own_a,) + second_a)
    out_a = to_owners(sent_a)

    right, left = first_b
    to_right = part_b[2] + right[:72]
    to_left = part_b[3] + left[:72]
    relay_right, cross_right = z_shift(to_right[:24], 2), z_shift(to_right[24:], 1)
    relay_left, cross_left = z_shift(to_left[:24], -2), z_shift(to_left[24:], -1)
    own_b = jnp.concatenate(
        [part_b[4][:24] + right[72:] + relay_left, part_b[4][24:] + left[72:] + relay_right], axis=0
    )
    out_b = to_owners(packed(1, sums_near, (own_b, cross_right, cross_left)))
    out = [
        got.reshape(32, 2, 2, cols).transpose(1, 2, 0, 3).reshape(2, 64 * cols) for got in (out_a, out_b)
    ]

    residual = jnp.concatenate(out, axis=0)
    occ_labels = jnp.arange(occ_energy.shape[0], dtype=jnp.int32)
    pair_hot = (pair_occ[:, :, None] == occ_labels[None, None, :]).astype(jnp.float32)
    pair_energy = jnp.sum(pair_hot * occ_energy[None, None, :], axis=(1, 2))
    update = residual / (ab_energy[None, :] - pair_energy[:, None])
    return (residual, update)


def solution(mesh):
    fine = Mesh(mesh.devices.reshape(2, 4, 4, 2, 4), GX + ("row",))
    return jax.shard_map(
        body,
        mesh=fine,
        in_specs=(
            P(GX, "row"),
            P("row", GX),
            P("row"),
            P(GX),
            P(),
            P(GX + ("row",), None),
            P(),
            P(),
        ),
        out_specs=(P(GX + ("row",), None), P(GX + ("row",), None)),
        check_vma=False,
    )
```
